32 devices in a mesh: ctx: 4 (over x, core), exp: 8 (over z, y).
Axes of the slice: x: 2, y: 2, z: 4, core: 2. Of those that a mesh axis runs over, the one named last changes fastest.
Arguments:
- queries: bfloat16 [8, 1024, 2048], P('exp', 'ctx'), may hold values from -5 to 5
- key_rows: bfloat16 [8, 1024, 2048], P('exp', 'ctx'), may hold values from -5 to 5
- value_rows: bfloat16 [8, 1024, 2048], P('exp', 'ctx'), may hold values from -6 to 6
- residual_in: bfloat16 [8, 1024, 2048], P('exp', 'ctx'), may hold values from -6 to 6
- norm_gain: float32 [2048], replicated, may hold values from 0.1 to 1.9
- routes: int32 [8, 1024, 2], P('exp', 'ctx'), may hold values from 0 to 7, all different within a row; in each aligned block of 256 rows (0 to 255, 256 to 511, ..., all dimensions but the last counted through in order) at most 80 rows name the same one
- gate_weights: float32 [8, 1024, 2], P('exp', 'ctx'), may hold values from 0.25 to 1
- gate_up_weight: bfloat16 [8, 2048, 2, 1024], P('exp', None, None, 'ctx'), may hold values from -0.125 to 0.125
- down_weight: bfloat16 [8, 1024, 2048], P('exp', 'ctx'), may hold values from -0.1875 to 0.1875
Outputs:
- layer_out: bfloat16 [8, 1024, 2048], P('exp', 'ctx')
The draws below stay inside these ranges and needn't reach their ends.
Inputs may be any that keep to these rules, and one draw needn't show every extreme that they name: `routes`: within the rows of one device (aligned blocks of 256 tokens in clip-then-frame order), no expert is named more than 80 times; the 2 experts of a token differ.
All inputs are finite; a program needn't handle non-finite values.
Results may differ from the reference program's by a relative error of at most 0.011.
Values may be sent and summed in bfloat16 or wider, within the bound.
A program may use at most 128 MiB of HBM per device.

```python
import math
import jax
import jax.numpy as jnp
import numpy as np
from jax import lax

HEADS = 16
HEAD = 128
D = 2048
FF = 1024
TOP = 2
TOK_DEV = 256
LEN = 1024
CLIPS = 8
EXPERTS = 8
CAP = 80
TOKENS = 8192
N_CTX = 4
N_EXP = 8


def draw_queries(key, part):
    result = jax.random.truncated_normal(jax.random.fold_in(key, 1), -5.0, 5.0, (CLIPS, LEN, D), jnp.float32)
    return result.astype(jnp.bfloat16)


def draw_key_rows(key, part):
    result = jax.random.truncated_normal(jax.random.fold_in(key, 2), -5.0, 5.0, (CLIPS, LEN, D), jnp.float32)
    return result.astype(jnp.bfloat16)


def level_of(key, extent, pieces, smallest, top_value):
    level = 1.0
    for dim, shards_of in pieces:
        draws = jax.random.uniform(jax.random.fold_in(jax.random.fold_in(key, 6), dim), (shards_of,), jnp.float32, smallest / len(pieces), top_value / len(pieces))
        level = level * jnp.repeat(jnp.exp(draws), extent[dim] // shards_of).reshape((-1,) + (1,) * (len(extent) - 1 - dim))
    return level


def shared_out(rng, own, number, rows, amount, top, limit, lean):
    order = jax.random.permutation(rng, amount)
    crowded, usual = portions_of(amount, rows * top, limit, lean, True), portions_of(amount, rows * top, limit, lean, False)
    places = jnp.arange(amount)

    def named(tallies, turn):
        used = int((tallies > 0).sum())
        fixed = max(1, used // 4)
        shifted = fixed + (places - fixed + turn * (used - fixed)) % max(1, amount - fixed)
        return jnp.zeros((amount,), jnp.int32).at[order[jnp.where(places < fixed, places, shifted)]].set(jnp.asarray(tallies, jnp.int32))

    tallies = jnp.where(number % 4 == 0, named(crowded, number // 4), named(usual, number - number // 4 - 1))
    mixed = jax.random.permutation(jax.random.fold_in(own, 3), amount)
    source_of, receiver = mixed[0:amount // 2 * 2:2], mixed[1:amount // 2 * 2:2]
    room = jnp.minimum(tallies[source_of] - 1, limit - tallies[receiver]) // 2
    room = jnp.where((source_of == order[0]) | (receiver == order[0]) | (tallies[receiver] == 0), 0, jnp.maximum(room, 0))
    shifted = jax.random.randint(jax.random.fold_in(own, 4), (amount // 2,), 0, 1 << 20) % (room + 1)
    tallies = tallies.at[source_of].add(-shifted).at[receiver].add(shifted)
    items = jnp.searchsorted(jnp.cumsum(tallies), jnp.arange(rows * top), side="right").astype(jnp.int32)
    grid = items.reshape(top, rows).T
    grid = grid[jax.random.permutation(jax.random.fold_in(own, 1), rows)]
    turn = jax.random.randint(jax.random.fold_in(own, 2), (rows, 1), 0, top)
    return jnp.take_along_axis(grid, (jnp.arange(top)[None, :] + turn) % top, axis=1)


def portions_of(number_of, total, limit, lean, full):
    loads = [(1 << 20) // math.isqrt(rank ** lean) + 1 for rank in range(1, number_of + 1)]
    largest = limit if full else min(limit, max(-(-total // number_of), total * loads[0] // sum(loads)))
    least = 1 if total - largest >= number_of - 1 else 0
    counts, surplus = [largest] + [least] * (number_of - 1), total - largest - least * (number_of - 1)
    while surplus > 0:
        free = [i for i in range(1, number_of) if counts[i] < largest] or [i for i in range(1, number_of) if counts[i] < limit]
        mass, left = sum([loads[i] for i in free]), surplus
        for i in free:
            more = min(limit - counts[i], max(1, left * loads[i] // mass), surplus)
            counts[i] = counts[i] + more
            surplus = surplus - more
    return np.array(counts)


def scatter_about(rng, dims, deviation, most, cuts=(), kind=jnp.bfloat16):
    gain = level_of(rng, dims, cuts, -0.22, 0.18) if cuts else 1.0
    drawn = jax.random.normal(rng, dims, jnp.float32) * deviation * gain
    return jnp.minimum(jnp.maximum(drawn, -most), most).astype(kind)


def setup_inputs(seed: int = 0) -> dict:
    keys = jax.random.split(jax.random.key(seed), 10)
    queries = draw_queries(jax.random.fold_in(keys[9], 71), 0)
    key_rows = draw_key_rows(jax.random.fold_in(keys[9], 71), 0)
    value_rows = scatter_about(keys[2], (CLIPS, LEN, D), 1.0, 6.0, ((0, 8), (1, 4)))
    residual_in = scatter_about(keys[3], (CLIPS, LEN, D), 1.0, 6.0, ((0, 8), (1, 4)))
    norm_gain = jnp.clip(1.0 + 0.18 * jax.random.normal(keys[4], (D,), jnp.float32), 0.1, 1.9)
    routes_keys = jax.random.split(jax.random.fold_in(keys[5], 1), CLIPS * LEN // TOK_DEV)
    routes_turns = jax.random.permutation(jax.random.fold_in(keys[5], 3), CLIPS * LEN // TOK_DEV)
    routes = jax.vmap(lambda own, number: shared_out(jax.random.fold_in(keys[5], 2), own, number, TOK_DEV, EXPERTS, TOP, CAP, 2))(routes_keys, routes_turns).reshape((CLIPS, LEN, TOP))
    gate_weights = jnp.clip(0.25 + 0.75 * jax.random.uniform(keys[6], (CLIPS, LEN, TOP), jnp.float32) ** level_of(keys[6], (CLIPS, LEN, TOP), ((0, 8), (1, 4)), -0.2, 0.2), 0.25, 1.0)
    gate_up_weight = scatter_about(keys[7], (EXPERTS, D, 2, FF), D ** -0.5, 0.125, ((0, 8), (3, 4)))
    down_weight = scatter_about(keys[8], (EXPERTS, FF, D), FF ** -0.5, 0.1875, ((0, 8), (1, 4)))
    return {"queries": queries, "key_rows": key_rows, "value_rows": value_rows, "residual_in": residual_in, "norm_gain": norm_gain, "routes": routes, "gate_weights": gate_weights, "gate_up_weight": gate_up_weight, "down_weight": down_weight}


def clip_attention(operands):
    query_part, key_part, value_part = operands
    query_heads = query_part.reshape(LEN, HEADS, HEAD).astype(jnp.float32)
    key_heads = key_part.reshape(LEN, HEADS, HEAD).astype(jnp.float32)
    value_heads = value_part.reshape(LEN, HEADS, HEAD).astype(jnp.float32)
    scores = jnp.einsum('qhd,khd->qhk', query_heads, key_heads) * HEAD ** (-0.5)
    row_max = lax.optimization_barrier(jnp.max(scores, axis=-1, keepdims=True))
    expo = jnp.exp(scores - row_max)
    row_total = lax.optimization_barrier(jnp.sum(expo, axis=-1))
    probs = lax.optimization_barrier(expo.astype(jnp.bfloat16)).astype(jnp.float32)
    weighted = jnp.einsum('qhk,khd->qhd', probs, value_heads)
    return (weighted / row_total[..., None]).reshape(LEN, D)

def reference(queries, key_rows, value_rows, residual_in, norm_gain, routes, gate_weights, gate_up_weight, down_weight):
    attention = lax.map(clip_attention, (queries, key_rows, value_rows))
    mixed_rows = (residual_in.astype(jnp.float32) + attention).astype(jnp.bfloat16)
    mixed_float = mixed_rows.astype(jnp.float32)
    mean_square = lax.optimization_barrier(jnp.mean(mixed_float * mixed_float, axis=-1, keepdims=True))
    normed = (mixed_float * lax.rsqrt(mean_square + 1e-05) * norm_gain).astype(jnp.bfloat16)
    flat_normed = normed.reshape(TOKENS, D)
    flat_routes = routes.reshape(TOKENS, TOP)
    flat_gates = gate_weights.reshape(TOKENS, TOP)
    max_rows = min(N_CTX * N_EXP * CAP, TOKENS)
    group_width = FF // N_CTX

    def one_expert(accumulated, expert_id):
        is_routed = flat_routes == expert_id
        weight = lax.optimization_barrier(jnp.sum(jnp.where(is_routed, flat_gates, 0.0), axis=1))
        sort_key = jnp.where(jnp.any(is_routed, axis=1), 0, 1).astype(jnp.int32)
        row_order = jnp.argsort(sort_key, stable=True)[:max_rows].astype(jnp.int32)
        picked = flat_normed[row_order]
        gate_and_up = jnp.dot(picked, gate_up_weight[expert_id].reshape(D, 2 * FF), preferred_element_type=jnp.float32)
        hidden = (jax.nn.silu(gate_and_up[:, :FF]) * gate_and_up[:, FF:]).astype(jnp.bfloat16)
        group_parts = jnp.einsum('rgf,gfd->grd', hidden.reshape(max_rows, N_CTX, group_width).astype(jnp.float32), down_weight[expert_id].reshape(N_CTX, group_width, D).astype(jnp.float32))
        group_parts = lax.optimization_barrier(group_parts.astype(jnp.bfloat16)).astype(jnp.float32)
        expert_out = lax.optimization_barrier(jnp.sum(group_parts, axis=0)).astype(jnp.bfloat16).astype(jnp.float32)
        accumulated = accumulated.at[row_order].add(weight[row_order][:, None] * expert_out)
        return (accumulated, None)
    expert_sum, _ = lax.scan(one_expert, jnp.zeros((TOKENS, D), jnp.float32), jnp.arange(EXPERTS, dtype=jnp.int32))
    result = (mixed_float.reshape(TOKENS, D) + expert_sum).astype(jnp.bfloat16)
    return result.reshape(CLIPS, LEN, D)
```

```python
import functools

import jax
import jax.numpy as jnp
from jax import lax
from jax.experimental import pallas as pl
from jax.experimental.pallas import tpu as pltpu
from jax.sharding import PartitionSpec as P

HEADS = 16
MESH = pl.DeviceIdType.MESH
F32 = jnp.float32
BF16 = jnp.bfloat16
OWN, CORE, CHIP, FAR = range(4)
TILE = 512


def flipped(index, offset, extent):
    result = jnp.int32(0)
    bit = 1
    while bit < extent:
        both = lax.div(index, jnp.int32(bit)) + lax.div(jnp.int32(offset), jnp.int32(bit))
        result = result + lax.rem(both, jnp.int32(2)) * bit
        bit *= 2
    return result


def rows_at(start, count):
    return pl.ds(pl.multiple_of(start, 16), count)


def columns_at(step, width):
    return pl.ds(pl.multiple_of(step * width, width), width)


def layer_kernel(
    n_exp, cap, chunk, scale,
    q_ref, k_ref, v_ref, residual_ref, gain_ref, routes_ref, routes_t_ref, gates_ref, gu_ref, dn_ref,
    out_ref,
    q_buf, k_buf, v_buf, residual_buf, mixed, normed, gu_buf, dn_buf,
    pick, place, send_buf, recv_buf, hidden, result_buf, back_buf,
    local_sem, kv_send, kv_recv, w_send, w_recv, out_send, out_recv, back_send, back_recv,
):
    tokens, features = q_ref.shape
    top = gates_ref.shape[1]
    units = dn_ref.shape[0]
    slots = send_buf.shape[0]
    chunks = features // chunk
    half = n_exp // 2
    half_rows = half * cap
    ctx = lax.axis_index("ctx")
    me = lax.axis_index("exp")
    core_peer = flipped(ctx, 1, 4)
    chip_peer = flipped(ctx, 2, 4)
    far_peer = flipped(ctx, 3, 4)

    local = [
        pltpu.make_async_copy(src, dst, local_sem.at[i])
        for i, (src, dst) in enumerate(
            [
                (q_ref, q_buf),
                (k_ref, k_buf.at[pl.ds(0, tokens)]),
                (v_ref, v_buf.at[pl.ds(0, tokens)]),
                (residual_ref, residual_buf),
                (gu_ref, gu_buf.at[OWN]),
                (dn_ref, dn_buf.at[pl.ds(0, units)]),
            ]
        )
    ]
    for copy in local:
        copy.start()

    barrier = pltpu.get_barrier_semaphore()
    for peer in (core_peer, chip_peer, far_peer):
        pl.semaphore_signal(barrier, inc=1, device_id={"ctx": peer}, device_id_type=MESH)

    @pl.loop(1, n_exp)
    def _(d):
        pl.semaphore_signal(
            barrier, inc=1, device_id={"exp": flipped(me, d, n_exp)}, device_id_type=MESH
        )

    pl.semaphore_wait(barrier, 3 + n_exp - 1)

    def kv_copy(kind, route, g):
        src, buf = ((k_ref, k_buf), (v_ref, v_buf))[kind]
        cols = columns_at(g, chunk)
        if route == FAR:
            block = buf.at[pl.ds(CHIP * tokens, tokens), cols]
        else:
            block = src.at[:, cols]
        return pltpu.make_async_remote_copy(
            src_ref=block,
            dst_ref=buf.at[pl.ds(route * tokens, tokens), cols],
            send_sem=kv_send.at[kind, route - 1, g],
            recv_sem=kv_recv.at[kind, route - 1, g],
            device_id={"ctx": chip_peer if route == CHIP else core_peer},
            device_id_type=MESH,
        )

    gu_pieces, dn_pieces = 4, 2
    pieces = gu_pieces + dn_pieces

    def weight_copy(route, i):
        if i < gu_pieces:
            size = features // gu_pieces
            part = pl.ds(i * size, size)
            src, dst = gu_ref.at[part], gu_buf.at[route, part]
            held = gu_buf.at[CHIP, part]
        else:
            size = units // dn_pieces
            start = (i - gu_pieces) * size
            src = dn_ref.at[pl.ds(start, size)]
            dst = dn_buf.at[pl.ds(route * units + start, size)]
            held = dn_buf.at[pl.ds(CHIP * units + start, size)]
        return pltpu.make_async_remote_copy(
            src_ref=held if route == FAR else src,
            dst_ref=dst,
            send_sem=w_send.at[route - 1, i],
            recv_sem=w_recv.at[route - 1, i],
            device_id={"ctx": chip_peer if route == CHIP else core_peer},
            device_id_type=MESH,
        )

    @pl.loop(0, chunks)
    def _(g):
        for kind in range(2):
            kv_copy(kind, CHIP, g).start()
            kv_copy(kind, CORE, g).start()

    for i in range(pieces):
        weight_copy(CORE, i).start()

    expert_lane = lax.broadcasted_iota(jnp.int32, (tokens, 128), 1)
    named = [routes_ref[:, j : j + 1] == expert_lane for j in range(top)]
    counted = sum(jnp.where(hit, 1.0, 0.0) for hit in named).astype(BF16)
    row = lax.broadcasted_iota(jnp.int32, (tokens, tokens), 0)
    col = lax.broadcasted_iota(jnp.int32, (tokens, tokens), 1)
    earlier = jnp.where(row > col, 1.0, 0.0).astype(BF16)
    slot = jnp.dot(earlier, counted, preferred_element_type=F32) + (expert_lane * cap).astype(F32)
    slot_lane = lax.broadcasted_iota(jnp.int32, (tokens, slots), 1).astype(F32)
    for j in range(top):
        target = jnp.sum(jnp.where(named[j], slot, 0.0), axis=1, keepdims=True)
        pick[j] = jnp.where(target == slot_lane, 1.0, 0.0).astype(BF16)

    expert_row = lax.broadcasted_iota(jnp.int32, (128, tokens), 0)
    named_t = [routes_t_ref[j : j + 1, :] == expert_row for j in range(top)]
    counted_t = sum(jnp.where(hit, 1.0, 0.0) for hit in named_t).astype(BF16)
    earlier_t = jnp.where(row < col, 1.0, 0.0).astype(BF16)
    slot_t = jnp.dot(counted_t, earlier_t, preferred_element_type=F32) + (expert_row * cap).astype(F32)
    slot_row = lax.broadcasted_iota(jnp.int32, (slots, tokens), 0).astype(F32)
    placed = jnp.zeros((slots, tokens), F32)
    for j in range(top):
        target = jnp.sum(jnp.where(named_t[j], slot_t, 0.0), axis=0, keepdims=True)
        placed = placed + jnp.where(target == slot_row, 1.0, 0.0)
    place[...] = placed.astype(BF16)

    for copy in local:
        copy.wait()

    @pl.loop(0, chunks + 1)
    def _(g):
        @pl.when(g < chunks)
        def _():
            for kind in range(2):
                kv_copy(kind, CHIP, g).wait_recv()
                kv_copy(kind, FAR, g).start()

        @pl.when(g == chunks - 2)
        def _():
            for i in range(pieces):
                weight_copy(CHIP, i).start()

        @pl.when(g > 0)
        def _():
            done = g - 1
            for kind in range(2):
                kv_copy(kind, CORE, done).wait_recv()
                kv_copy(kind, FAR, done).wait_recv()
            for h in range(chunk // 128):
                cols = pl.ds(pl.multiple_of(done * chunk + h * 128, 128), 128)
                scores = (
                    lax.dot_general(
                        q_buf[:, cols], k_buf[:, cols], (((1,), (1,)), ((), ())),
                        preferred_element_type=F32,
                    )
                    * scale
                )
                expo = jnp.exp(scores - jnp.max(scores, axis=1, keepdims=True))
                total = jnp.sum(expo, axis=1, keepdims=True)
                weighted = jnp.dot(expo.astype(BF16), v_buf[:, cols], preferred_element_type=F32)
                mixed[:, cols] = (residual_buf[:, cols].astype(F32) + weighted / total).astype(BF16)

    @pl.loop(0, tokens // 32)
    def _(i):
        part = rows_at(i * 32, 32)
        value = mixed[part, :].astype(F32)
        mean_square = jnp.mean(value * value, axis=1, keepdims=True)
        normed[part, :] = (value * lax.rsqrt(mean_square + 1e-05) * gain_ref[...]).astype(BF16)

    def out_copy(d):
        return pltpu.make_async_remote_copy(
            src_ref=send_buf.at[rows_at(flipped(me, d, n_exp) * cap, cap)],
            dst_ref=recv_buf.at[rows_at(d * cap, cap)],
            send_sem=out_send.at[d],
            recv_sem=out_recv.at[d],
            device_id={"exp": flipped(me, d, n_exp)},
            device_id_type=MESH,
        )

    def back_copy(d):
        return pltpu.make_async_remote_copy(
            src_ref=result_buf.at[rows_at(d * cap, cap)],
            dst_ref=back_buf.at[rows_at(me * cap, cap)],
            send_sem=back_send.at[d],
            recv_sem=back_recv.at[d],
            device_id={"exp": flipped(me, d, n_exp)},
            device_id_type=MESH,
        )

    my_half = lax.div(me, jnp.int32(half))
    for which in (1, 0):
        part = rows_at(lax.rem(my_half + which, jnp.int32(2)) * half_rows, half_rows)

        @pl.loop(0, features // TILE)
        def _(t):
            cols = columns_at(t, TILE)
            send_buf[part, cols] = jnp.dot(
                place[part, :], normed[:, cols], preferred_element_type=F32
            ).astype(BF16)

        @pl.loop(max(1, which * half), which * half + half)
        def _(d):
            out_copy(d).start()

    recv_buf[pl.ds(0, cap), :] = send_buf[rows_at(me * cap, cap), :]

    for i in range(pieces):
        weight_copy(CHIP, i).wait_recv()
        weight_copy(FAR, i).start()
    for i in range(pieces):
        weight_copy(CORE, i).wait_recv()
        weight_copy(FAR, i).wait_recv()

    for which in (0, 1):
        part = pl.ds(which * half_rows, half_rows)

        @pl.loop(max(1, which * half), which * half + half)
        def _(d):
            out_copy(d).wait_recv()

        @pl.loop(0, 4)
        def _(r):
            both = jnp.dot(recv_buf[part, :], gu_buf[r], preferred_element_type=F32)
            gate, up = both[:, :units], both[:, units:]
            hidden[:, columns_at(r, units)] = (gate / (1.0 + jnp.exp(-gate)) * up).astype(BF16)

        @pl.loop(0, features // TILE)
        def _(t):
            cols = columns_at(t, TILE)
            result_buf[part, cols] = jnp.dot(
                hidden[...], dn_buf[:, cols], preferred_element_type=F32
            ).astype(BF16)

        @pl.loop(max(1, which * half), which * half + half)
        def _(d):
            back_copy(d).start()

    back_buf[rows_at(me * cap, cap), :] = result_buf[pl.ds(0, cap), :]

    @pl.loop(1, n_exp)
    def _(d):
        back_copy(d).wait_recv()

    @pl.loop(0, features // TILE)
    def _(t):
        cols = columns_at(t, TILE)
        total = mixed[:, cols].astype(F32)
        for j in range(top):
            routed = jnp.dot(pick[j], back_buf[:, cols], preferred_element_type=F32)
            total = total + gates_ref[:, j : j + 1] * routed
        out_ref[:, cols] = total.astype(BF16)

    @pl.loop(1, n_exp)
    def _(d):
        out_copy(d).wait_send()
        back_copy(d).wait_send()

    @pl.loop(0, chunks)
    def _(g):
        for kind in range(2):
            for route in (CORE, CHIP, FAR):
                kv_copy(kind, route, g).wait_send()

    for i in range(pieces):
        for route in (CORE, CHIP, FAR):
            weight_copy(route, i).wait_send()


def shards(
    queries,
    key_rows,
    value_rows,
    residual_in,
    norm_gain,
    routes,
    gate_weights,
    gate_up_weight,
    down_weight,
):
    clip_count, row_count, feature_count = queries.shape
    tokens = clip_count * row_count
    top = routes.shape[-1]
    n_exp = lax.axis_size("exp")
    n_ctx = lax.axis_size("ctx")
    units = down_weight.shape[1]
    assert clip_count == 1 and n_ctx == 4 and gate_up_weight.shape[0] == 1
    assert n_exp & (n_exp - 1) == 0 and feature_count == HEADS * 128
    capacity = max(2, -(-(5 * tokens * top) // (4 * n_exp)))
    cap = -(-capacity // 16) * 16
    slots = n_exp * cap
    chunk = 256
    chunks = feature_count // chunk
    flat = (tokens, feature_count)
    flat_routes = routes.reshape(tokens, top)
    anywhere = pl.BlockSpec(memory_space=pl.ANY)
    vmem = pl.BlockSpec(memory_space=pltpu.VMEM)
    dma = pltpu.SemaphoreType.DMA
    out = pl.pallas_call(
        functools.partial(layer_kernel, n_exp, cap, chunk, (feature_count // HEADS) ** (-0.5)),
        out_shape=jax.ShapeDtypeStruct(flat, BF16),
        in_specs=[anywhere] * 4 + [vmem] * 4 + [anywhere] * 2,
        out_specs=vmem,
        scratch_shapes=[
            pltpu.VMEM(flat, BF16),
            pltpu.VMEM((n_ctx * tokens, feature_count), BF16),
            pltpu.VMEM((n_ctx * tokens, feature_count), BF16),
            pltpu.VMEM(flat, BF16),
            pltpu.VMEM(flat, BF16),
            pltpu.VMEM(flat, BF16),
            pltpu.VMEM((n_ctx, feature_count, 2 * units), BF16),
            pltpu.VMEM((n_ctx * units, feature_count), BF16),
            pltpu.VMEM((top, tokens, slots), BF16),
            pltpu.VMEM((slots, tokens), BF16),
            pltpu.VMEM((slots, feature_count), BF16),
            pltpu.VMEM((slots, feature_count), BF16),
            pltpu.VMEM((slots // 2, n_ctx * units), BF16),
            pltpu.VMEM((slots, feature_count), BF16),
            pltpu.VMEM((slots, feature_count), BF16),
            dma((6,)),
            dma((2, 3, chunks)),
            dma((2, 3, chunks)),
            dma((3, 6)),
            dma((3, 6)),
            dma((n_exp,)),
            dma((n_exp,)),
            dma((n_exp,)),
            dma((n_exp,)),
        ],
        compiler_params=pltpu.CompilerParams(
            collective_id=0, has_side_effects=True, vmem_limit_bytes=60 * 1024 * 1024
        ),
        cost_estimate=pl.CostEstimate(
            flops=10_000_000_000, bytes_accessed=20_000_000, transcendentals=5_000_000
        ),
    )(
        queries.reshape(flat),
        key_rows.reshape(flat),
        value_rows.reshape(flat),
        residual_in.reshape(flat),
        norm_gain.reshape(1, feature_count),
        flat_routes,
        flat_routes.T,
        gate_weights.reshape(tokens, top),
        gate_up_weight.reshape(feature_count, 2 * units),
        down_weight.reshape(units, feature_count),
    )
    return out.reshape(clip_count, row_count, feature_count)


def solution(mesh):
    return jax.shard_map(
        shards,
        mesh=mesh,
        in_specs=(
            P("exp", "ctx", None),
            P("exp", "ctx", None),
            P("exp", "ctx", None),
            P("exp", "ctx", None),
            P(),
            P("exp", "ctx", None),
            P("exp", "ctx", None),
            P("exp", None, None, "ctx"),
            P("exp", "ctx", None),
        ),
        out_specs=P("exp", "ctx", None),
        check_vma=False,
    )
```

```python
import functools

import jax
import jax.numpy as jnp
from jax import lax
from jax.experimental import pallas as pl
from jax.experimental.pallas import tpu as pltpu
from jax.sharding import PartitionSpec as P

HEADS = 16
MESH = pl.DeviceIdType.MESH
F32 = jnp.float32
BF16 = jnp.bfloat16
OWN, CORE, CHIP, FAR = range(4)
TILE = 512


def flipped(index, offset, extent):
    result = jnp.int32(0)
    bit = 1
    while bit < extent:
        both = lax.div(index, jnp.int32(bit)) + lax.div(jnp.int32(offset), jnp.int32(bit))
        result = result + lax.rem(both, jnp.int32(2)) * bit
        bit *= 2
    return result


def rows_at(start, count):
    return pl.ds(pl.multiple_of(start, 16), count)


def columns_at(step, width):
    return pl.ds(pl.multiple_of(step * width, width), width)


def layer_kernel(
    n_exp, cap, chunk, scale,
    q_ref, k_ref, v_ref, residual_ref, gain_ref, routes_ref, gates_ref, gu_ref, dn_ref,
    out_ref,
    q_buf, k_buf, v_buf, residual_buf, mixed, gu_buf, dn_buf,
    pick, place, gate_column, send_buf, recv_buf, hidden, result_buf, back_buf,
    local_sem, kv_send, kv_recv, w_send, w_recv, out_send, out_recv, back_send, back_recv,
):
    tokens, features = q_ref.shape
    top = gates_ref.shape[0]
    units = dn_ref.shape[0]
    slots = send_buf.shape[0]
    chunks = features // chunk
    half = n_exp // 2
    half_rows = half * cap
    ctx = lax.axis_index("ctx")
    me = lax.axis_index("exp")
    core_peer = flipped(ctx, 1, 4)
    chip_peer = flipped(ctx, 2, 4)
    far_peer = flipped(ctx, 3, 4)

    local = [
        pltpu.make_async_copy(src, dst, local_sem.at[i])
        for i, (src, dst) in enumerate(
            [
                (q_ref, q_buf),
                (k_ref, k_buf.at[pl.ds(0, tokens)]),
                (v_ref, v_buf.at[pl.ds(0, tokens)]),
                (residual_ref, residual_buf),
                (gu_ref, gu_buf.at[OWN]),
                (dn_ref, dn_buf.at[pl.ds(0, units)]),
            ]
        )
    ]
    for copy in local:
        copy.start()

    barrier = pltpu.get_barrier_semaphore()
    for peer in (core_peer, chip_peer, far_peer):
        pl.semaphore_signal(barrier, inc=1, device_id={"ctx": peer}, device_id_type=MESH)

    @pl.loop(1, n_exp)
    def _(d):
        pl.semaphore_signal(
            barrier, inc=1, device_id={"exp": flipped(me, d, n_exp)}, device_id_type=MESH
        )

    pl.semaphore_wait(barrier, 3 + n_exp - 1)

    def kv_copy(kind, route, g):
        src, buf = ((k_ref, k_buf), (v_ref, v_buf))[kind]
        cols = columns_at(g, chunk)
        if route == FAR:
            block = buf.at[pl.ds(CHIP * tokens, tokens), cols]
        else:
            block = src.at[:, cols]
        return pltpu.make_async_remote_copy(
            src_ref=block,
            dst_ref=buf.at[pl.ds(route * tokens, tokens), cols],
            send_sem=kv_send.at[kind, route - 1, g],
            recv_sem=kv_recv.at[kind, route - 1, g],
            device_id={"ctx": chip_peer if route == CHIP else core_peer},
            device_id_type=MESH,
        )

    gu_pieces, dn_pieces = 4, features // TILE
    pieces = gu_pieces + dn_pieces

    def weight_copy(route, i):
        if i < gu_pieces:
            size = features // gu_pieces
            part = pl.ds(i * size, size)
            src, dst = gu_ref.at[part], gu_buf.at[route, part]
            held = gu_buf.at[CHIP, part]
        else:
            cols = pl.ds((i - gu_pieces) * TILE, TILE)
            src = dn_ref.at[:, cols]
            dst = dn_buf.at[pl.ds(route * units, units), cols]
            held = dn_buf.at[pl.ds(CHIP * units, units), cols]
        return pltpu.make_async_remote_copy(
            src_ref=held if route == FAR else src,
            dst_ref=dst,
            send_sem=w_send.at[route - 1, i],
            recv_sem=w_recv.at[route - 1, i],
            device_id={"ctx": chip_peer if route == CHIP else core_peer},
            device_id_type=MESH,
        )

    @pl.loop(0, chunks)
    def _(g):
        for kind in range(2):
            kv_copy(kind, CHIP, g).start()
            kv_copy(kind, CORE, g).start()

    for i in range(pieces):
        weight_copy(CORE, i).start()

    expert_row = lax.broadcasted_iota(jnp.int32, (128, tokens), 0)
    named = [routes_ref[j : j + 1, :] == expert_row for j in range(top)]
    counted = sum(jnp.where(hit, 1.0, 0.0) for hit in named).astype(BF16)
    row = lax.broadcasted_iota(jnp.int32, (tokens, tokens), 0)
    col = lax.broadcasted_iota(jnp.int32, (tokens, tokens), 1)
    earlier = jnp.where(row < col, 1.0, 0.0).astype(BF16)
    slot = jnp.dot(counted, earlier, preferred_element_type=F32) + (expert_row * cap).astype(F32)
    slot_row = lax.broadcasted_iota(jnp.int32, (slots, tokens), 0).astype(F32)
    slot_lane = lax.broadcasted_iota(jnp.int32, (tokens, slots), 1).astype(F32)
    placed = jnp.zeros((slots, tokens), F32)
    for j in range(top):
        target = jnp.sum(jnp.where(named[j], slot, 0.0), axis=0, keepdims=True)
        placed = placed + jnp.where(target == slot_row, 1.0, 0.0)
        target = jnp.sum(jnp.where(row == col, target, 0.0), axis=1, keepdims=True)
        pick[j] = jnp.where(target == slot_lane, 1.0, 0.0).astype(BF16)
        gate = jnp.sum(jnp.where(row == col, gates_ref[j : j + 1, :], 0.0), axis=1, keepdims=True)
        gate_column[j] = jnp.broadcast_to(gate, (tokens, 128))
    place[...] = placed.astype(BF16)

    for copy in local:
        copy.wait()

    def out_copy(d, cols=slice(None)):
        return pltpu.make_async_remote_copy(
            src_ref=send_buf.at[rows_at(flipped(me, d, n_exp) * cap, cap), cols],
            dst_ref=recv_buf.at[rows_at(d * cap, cap), cols],
            send_sem=out_send.at[d],
            recv_sem=out_recv.at[d],
            device_id={"exp": flipped(me, d, n_exp)},
            device_id_type=MESH,
        )

    def back_copy(d, t):
        cols = columns_at(t, TILE)
        return pltpu.make_async_remote_copy(
            src_ref=result_buf.at[rows_at(d * cap, cap), cols],
            dst_ref=back_buf.at[rows_at(me * cap, cap), cols],
            send_sem=back_send.at[d, t],
            recv_sem=back_recv.at[d, t],
            device_id={"exp": flipped(me, d, n_exp)},
            device_id_type=MESH,
        )

    @pl.loop(0, chunks + 1)
    def _(g):
        @pl.when(g < chunks)
        def _():
            for kind in range(2):
                kv_copy(kind, CHIP, g).wait_recv()
                kv_copy(kind, FAR, g).start()

        @pl.when(g == chunks - 2)
        def _():
            for i in range(pieces):
                weight_copy(CHIP, i).start()

        @pl.when(g > 0)
        def _():
            done = g - 1
            for kind in range(2):
                kv_copy(kind, CORE, done).wait_recv()
                kv_copy(kind, FAR, done).wait_recv()
            for h in range(chunk // 128):
                cols = pl.ds(pl.multiple_of(done * chunk + h * 128, 128), 128)
                scores = (
                    lax.dot_general(
                        q_buf[:, cols], k_buf[:, cols], (((1,), (1,)), ((), ())),
                        preferred_element_type=F32,
                    )
                    * scale
                )
                expo = jnp.exp(scores - jnp.max(scores, axis=1, keepdims=True))
                total = jnp.sum(expo, axis=1, keepdims=True)
                weighted = jnp.dot(expo.astype(BF16), v_buf[:, cols], preferred_element_type=F32)
                mixed[:, cols] = (residual_buf[:, cols].astype(F32) + weighted / total).astype(BF16)

            cols = columns_at(done, chunk)
            send_buf[:, cols] = jnp.dot(
                place[...], mixed[:, cols], preferred_element_type=F32
            ).astype(BF16)

            @pl.loop(1, n_exp)
            def _(d):
                out_copy(n_exp - d, cols).start()

    recv_buf[pl.ds(0, cap), :] = send_buf[rows_at(me * cap, cap), :]

    @pl.loop(1, n_exp)
    def _(d):
        out_copy(d).wait_recv()

    @pl.loop(0, slots // 16)
    def _(i):
        part = rows_at(i * 16, 16)
        value = recv_buf[part, :].astype(F32)
        mean_square = jnp.mean(value * value, axis=1, keepdims=True)
        recv_buf[part, :] = (value * lax.rsqrt(mean_square + 1e-05) * gain_ref[...]).astype(BF16)

    def expert_hidden(r):
        both = jnp.dot(recv_buf[...], gu_buf[r], preferred_element_type=F32)
        gate, up = both[:, :units], both[:, units:]
        hidden[:, columns_at(r, units)] = (gate / (1.0 + jnp.exp(-gate)) * up).astype(BF16)

    for i in range(gu_pieces):
        weight_copy(CORE, i).wait_recv()
    pl.loop(OWN, CHIP)(expert_hidden)
    for i in range(gu_pieces):
        weight_copy(CHIP, i).wait_recv()
        weight_copy(FAR, i).start()
    pl.loop(CHIP, CHIP + 1)(expert_hidden)
    for i in range(gu_pieces):
        weight_copy(FAR, i).wait_recv()
    pl.loop(FAR, FAR + 1)(expert_hidden)

    for t in range(dn_pieces):
        weight_copy(CHIP, gu_pieces + t).wait_recv()
        weight_copy(FAR, gu_pieces + t).start()
        weight_copy(CORE, gu_pieces + t).wait_recv()
        weight_copy(FAR, gu_pieces + t).wait_recv()
        cols = pl.ds(t * TILE, TILE)
        for which in (1, 0):
            part = pl.ds(which * half_rows, half_rows)
            result_buf[part, cols] = jnp.dot(
                hidden[part, :], dn_buf[:, cols], preferred_element_type=F32
            ).astype(BF16)

            @pl.loop(max(1, which * half), which * half + half)
            def _(d):
                back_copy(d, t).start()

    back_buf[rows_at(me * cap, cap), :] = result_buf[pl.ds(0, cap), :]

    @pl.loop(0, dn_pieces)
    def _(t):
        @pl.loop(1, n_exp)
        def _(d):
            back_copy(d, t).wait_recv()

        cols = columns_at(t, TILE)
        total = mixed[:, cols].astype(F32)
        for j in range(top):
            routed = jnp.dot(pick[j], back_buf[:, cols], preferred_element_type=F32)
            total = total + gate_column[j, :, 0:1] * routed
        out_ref[:, cols] = total.astype(BF16)

    @pl.loop(1, n_exp)
    def _(d):
        out_copy(d).wait_send()
        for t in range(dn_pieces):
            back_copy(d, t).wait_send()

    @pl.loop(0, chunks)
    def _(g):
        for kind in range(2):
            for route in (CORE, CHIP, FAR):
                kv_copy(kind, route, g).wait_send()

    for i in range(pieces):
        for route in (CORE, CHIP, FAR):
            weight_copy(route, i).wait_send()


def shards(
    queries,
    key_rows,
    value_rows,
    residual_in,
    norm_gain,
    routes,
    gate_weights,
    gate_up_weight,
    down_weight,
):
    clip_count, row_count, feature_count = queries.shape
    tokens = clip_count * row_count
    top = routes.shape[-1]
    n_exp = lax.axis_size("exp")
    n_ctx = lax.axis_size("ctx")
    units = down_weight.shape[1]
    assert clip_count == 1 and n_ctx == 4 and gate_up_weight.shape[0] == 1
    assert n_exp & (n_exp - 1) == 0 and feature_count == HEADS * 128
    capacity = max(2, -(-(5 * tokens * top) // (4 * n_exp)))
    cap = -(-capacity // 16) * 16
    slots = n_exp * cap
    chunk = 256
    chunks = feature_count // chunk
    tiles = feature_count // TILE
    flat = (tokens, feature_count)
    anywhere = pl.BlockSpec(memory_space=pl.ANY)
    vmem = pl.BlockSpec(memory_space=pltpu.VMEM)
    dma = pltpu.SemaphoreType.DMA
    out = pl.pallas_call(
        functools.partial(layer_kernel, n_exp, cap, chunk, (feature_count // HEADS) ** (-0.5)),
        out_shape=jax.ShapeDtypeStruct(flat, BF16),
        in_specs=[anywhere] * 4 + [vmem] * 3 + [anywhere] * 2,
        out_specs=vmem,
        scratch_shapes=[
            pltpu.VMEM(flat, BF16),
            pltpu.VMEM((n_ctx * tokens, feature_count), BF16),
            pltpu.VMEM((n_ctx * tokens, feature_count), BF16),
            pltpu.VMEM(flat, BF16),
            pltpu.VMEM(flat, BF16),
            pltpu.VMEM((n_ctx, feature_count, 2 * units), BF16),
            pltpu.VMEM((n_ctx * units, feature_count), BF16),
            pltpu.VMEM((top, tokens, slots), BF16),
            pltpu.VMEM((slots, tokens), BF16),
            pltpu.VMEM((top, tokens, 128), F32),
            pltpu.VMEM((slots, feature_count), BF16),
            pltpu.VMEM((slots, feature_count), BF16),
            pltpu.VMEM((slots, n_ctx * units), BF16),
            pltpu.VMEM((slots, feature_count), BF16),
            pltpu.VMEM((slots, feature_count), BF16),
            dma((6,)),
            dma((2, 3, chunks)),
            dma((2, 3, chunks)),
            dma((3, 4 + tiles)),
            dma((3, 4 + tiles)),
            dma((n_exp,)),
            dma((n_exp,)),
            dma((n_exp, tiles)),
            dma((n_exp, tiles)),
        ],
        compiler_params=pltpu.CompilerParams(
            collective_id=0, has_side_effects=True, vmem_limit_bytes=60 * 1024 * 1024
        ),
        cost_estimate=pl.CostEstimate(
            flops=10_000_000_000, bytes_accessed=20_000_000, transcendentals=5_000_000
        ),
    )(
        queries.reshape(flat),
        key_rows.reshape(flat),
        value_rows.reshape(flat),
        residual_in.reshape(flat),
        norm_gain.reshape(1, feature_count),
        routes.reshape(tokens, top).T,
        gate_weights.reshape(tokens, top).T,
        gate_up_weight.reshape(feature_count, 2 * units),
        down_weight.reshape(units, feature_count),
    )
    return out.reshape(clip_count, row_count, feature_count)


def solution(mesh):
    return jax.shard_map(
        shards,
        mesh=mesh,
        in_specs=(
            P("exp", "ctx", None),
            P("exp", "ctx", None),
            P("exp", "ctx", None),
            P("exp", "ctx", None),
            P(),
            P("exp", "ctx", None),
            P("exp", "ctx", None),
            P("exp", None, None, "ctx"),
            P("exp", "ctx", None),
        ),
        out_specs=P("exp", "ctx", None),
        check_vma=False,
    )
```

```python
import functools

import jax
import jax.numpy as jnp
from jax import lax
from jax.experimental import pallas as pl
from jax.experimental.pallas import tpu as pltpu
from jax.sharding import PartitionSpec as P

HEADS = 16
MESH = pl.DeviceIdType.MESH
F32 = jnp.float32
BF16 = jnp.bfloat16
OWN, CORE, CHIP, FAR = range(4)
TILE = 512


def flipped(index, offset, extent):
    result = jnp.int32(0)
    bit = 1
    while bit < extent:
        both = lax.div(index, jnp.int32(bit)) + lax.div(jnp.int32(offset), jnp.int32(bit))
        result = result + lax.rem(both, jnp.int32(2)) * bit
        bit *= 2
    return result


def rows_at(start, count):
    return pl.ds(pl.multiple_of(start, 16), count)


def columns_at(step, width):
    return pl.ds(pl.multiple_of(step * width, width), width)


def layer_kernel(
    n_exp, cap, chunk, scale,
    q_ref, k_ref, v_ref, residual_ref, gain_ref, routes_ref, gates_ref, gu_ref, dn_ref,
    out_ref,
    q_buf, k_buf, v_buf, residual_buf, mixed, raw_buf, gu_buf, dn_buf,
    pick, place, gate_column, send_buf, recv_buf, hidden, result_buf, back_buf,
    local_sem, kv_send, kv_recv, w_send, w_recv, out_send, out_recv, back_send, back_recv,
):
    tokens, features = q_ref.shape
    top = gates_ref.shape[0]
    units = dn_ref.shape[0]
    half_units = units // 2
    slots = send_buf.shape[0]
    chunks = features // chunk
    half = n_exp // 2
    half_rows = half * cap
    ctx = lax.axis_index("ctx")
    me = lax.axis_index("exp")
    core_peer = flipped(ctx, 1, 4)
    chip_peer = flipped(ctx, 2, 4)
    far_peer = flipped(ctx, 3, 4)

    local = [
        pltpu.make_async_copy(src, dst, local_sem.at[i])
        for i, (src, dst) in enumerate(
            [
                (q_ref, q_buf),
                (k_ref, k_buf.at[pl.ds(0, tokens)]),
                (v_ref, v_buf.at[pl.ds(0, tokens)]),
                (residual_ref, residual_buf),
                (gu_ref, raw_buf),
                (dn_ref, dn_buf.at[pl.ds(0, units)]),
            ]
        )
    ]
    for copy in local:
        copy.start()

    barrier = pltpu.get_barrier_semaphore()
    for peer in (core_peer, chip_peer, far_peer):
        pl.semaphore_signal(barrier, inc=1, device_id={"ctx": peer}, device_id_type=MESH)

    @pl.loop(1, n_exp)
    def _(d):
        pl.semaphore_signal(
            barrier, inc=1, device_id={"exp": flipped(me, d, n_exp)}, device_id_type=MESH
        )

    pl.semaphore_wait(barrier, 3 + n_exp - 1)

    def kv_copy(kind, route, g):
        src, buf = ((k_ref, k_buf), (v_ref, v_buf))[kind]
        cols = columns_at(g, chunk)
        if route == FAR:
            block = buf.at[pl.ds(CHIP * tokens, tokens), cols]
        else:
            block = src.at[:, cols]
        return pltpu.make_async_remote_copy(
            src_ref=block,
            dst_ref=buf.at[pl.ds(route * tokens, tokens), cols],
            send_sem=kv_send.at[kind, route - 1, g],
            recv_sem=kv_recv.at[kind, route - 1, g],
            device_id={"ctx": chip_peer if route == CHIP else core_peer},
            device_id_type=MESH,
        )

    gu_pieces, dn_pieces = 4, features // TILE
    pieces = gu_pieces + dn_pieces

    def weight_copy(route, i):
        if i < gu_pieces:
            part = pl.ds(i % 2 * (features // 2), features // 2)
            cols = pl.ds(i // 2 * units, units)
            src, dst = gu_buf.at[OWN, part, cols], gu_buf.at[route, part, cols]
            held = gu_buf.at[CHIP, part, cols]
        else:
            cols = pl.ds((i - gu_pieces) * TILE, TILE)
            src = dn_ref.at[:, cols]
            dst = dn_buf.at[pl.ds(route * units, units), cols]
            held = dn_buf.at[pl.ds(CHIP * units, units), cols]
        return pltpu.make_async_remote_copy(
            src_ref=held if route == FAR else src,
            dst_ref=dst,
            send_sem=w_send.at[route - 1, i],
            recv_sem=w_recv.at[route - 1, i],
            device_id={"ctx": chip_peer if route == CHIP else core_peer},
            device_id_type=MESH,
        )

    @pl.loop(0, chunks)
    def _(g):
        for kind in range(2):
            kv_copy(kind, CHIP, g).start()
            kv_copy(kind, CORE, g).start()

    local[4].wait()

    @pl.loop(0, features // 128)
    def _(i):
        part = rows_at(i * 128, 128)
        for j in range(2):
            value = raw_buf[part, j, :]
            for h in range(2):
                gu_buf[OWN, part, h * units + j * half_units : h * units + (j + 1) * half_units] = (
                    value[:, h * half_units : (h + 1) * half_units]
                )

    for i in range(pieces):
        weight_copy(CORE, i).start()

    expert_row = lax.broadcasted_iota(jnp.int32, (128, tokens), 0)
    named = [routes_ref[j : j + 1, :] == expert_row for j in range(top)]
    counted = sum(jnp.where(hit, 1.0, 0.0) for hit in named).astype(BF16)
    row = lax.broadcasted_iota(jnp.int32, (tokens, tokens), 0)
    col = lax.broadcasted_iota(jnp.int32, (tokens, tokens), 1)
    earlier = jnp.where(row < col, 1.0, 0.0).astype(BF16)
    slot = jnp.dot(counted, earlier, preferred_element_type=F32) + (expert_row * cap).astype(F32)
    slot_row = lax.broadcasted_iota(jnp.int32, (slots, tokens), 0).astype(F32)
    slot_lane = lax.broadcasted_iota(jnp.int32, (tokens, slots), 1).astype(F32)
    placed = jnp.zeros((slots, tokens), F32)
    for j in range(top):
        target = jnp.sum(jnp.where(named[j], slot, 0.0), axis=0, keepdims=True)
        placed = placed + jnp.where(target == slot_row, 1.0, 0.0)
        target = jnp.sum(jnp.where(row == col, target, 0.0), axis=1, keepdims=True)
        pick[j] = jnp.where(target == slot_lane, 1.0, 0.0).astype(BF16)
        gate = jnp.sum(jnp.where(row == col, gates_ref[j : j + 1, :], 0.0), axis=1, keepdims=True)
        gate_column[j] = jnp.broadcast_to(gate, (tokens, 128))
    place[...] = placed.astype(BF16)

    for i in (0, 1, 2, 3, 5):
        local[i].wait()

    def out_copy(d, cols=slice(None)):
        return pltpu.make_async_remote_copy(
            src_ref=send_buf.at[rows_at(flipped(me, d, n_exp) * cap, cap), cols],
            dst_ref=recv_buf.at[rows_at(d * cap, cap), cols],
            send_sem=out_send.at[d],
            recv_sem=out_recv.at[d],
            device_id={"exp": flipped(me, d, n_exp)},
            device_id_type=MESH,
        )

    def back_copy(d, t):
        cols = columns_at(t, TILE)
        return pltpu.make_async_remote_copy(
            src_ref=result_buf.at[rows_at(d * cap, cap), cols],
            dst_ref=back_buf.at[rows_at(me * cap, cap), cols],
            send_sem=back_send.at[d, t],
            recv_sem=back_recv.at[d, t],
            device_id={"exp": flipped(me, d, n_exp)},
            device_id_type=MESH,
        )

    @pl.loop(0, chunks + 1)
    def _(g):
        @pl.when(g < chunks)
        def _():
            for kind in range(2):
                kv_copy(kind, CHIP, g).wait_recv()
                kv_copy(kind, FAR, g).start()

        for i in range(pieces):

            @pl.when(g == min(2 + i, chunks - 2))
            def _():
                weight_copy(CHIP, i).start()

        @pl.when(g > 0)
        def _():
            done = g - 1
            for kind in range(2):
                kv_copy(kind, CORE, done).wait_recv()
                kv_copy(kind, FAR, done).wait_recv()
            for h in range(chunk // 128):
                cols = pl.ds(pl.multiple_of(done * chunk + h * 128, 128), 128)
                scores = (
                    lax.dot_general(
                        q_buf[:, cols], k_buf[:, cols], (((1,), (1,)), ((), ())),
                        preferred_element_type=F32,
                    )
                    * scale
                )
                expo = jnp.exp(scores - jnp.max(scores, axis=1, keepdims=True))
                total = jnp.sum(expo, axis=1, keepdims=True)
                weighted = jnp.dot(expo.astype(BF16), v_buf[:, cols], preferred_element_type=F32)
                mixed[:, cols] = (residual_buf[:, cols].astype(F32) + weighted / total).astype(BF16)

            cols = columns_at(done, chunk)
            send_buf[:, cols] = jnp.dot(
                place[...], mixed[:, cols], preferred_element_type=F32
            ).astype(BF16)

            @pl.loop(1, n_exp)
            def _(d):
                out_copy(n_exp - d, cols).start()

    recv_buf[pl.ds(0, cap), :] = send_buf[rows_at(me * cap, cap), :]

    @pl.loop(1, n_exp)
    def _(d):
        out_copy(d).wait_recv()

    @pl.loop(0, slots // 16)
    def _(i):
        part = rows_at(i * 16, 16)
        value = recv_buf[part, :].astype(F32)
        mean_square = jnp.mean(value * value, axis=1, keepdims=True)
        recv_buf[part, :] = (value * lax.rsqrt(mean_square + 1e-05) * gain_ref[...]).astype(BF16)

    def expert_hidden(r, h):
        both = jnp.dot(
            recv_buf[...], gu_buf[r, :, h * units : (h + 1) * units], preferred_element_type=F32
        )
        gate, up = both[:, :half_units], both[:, half_units:]
        cols = columns_at(2 * r + h, half_units)
        hidden[:, cols] = (gate / (1.0 + jnp.exp(-gate)) * up).astype(BF16)

    for i in range(gu_pieces):
        weight_copy(CORE, i).wait_recv()

    @pl.loop(OWN, CHIP)
    def _(r):
        expert_hidden(r, 0)
        expert_hidden(r, 1)

    for h in range(2):
        for i in (2 * h, 2 * h + 1):
            weight_copy(CHIP, i).wait_recv()
            weight_copy(FAR, i).start()
        pl.loop(CHIP, CHIP + 1)(functools.partial(expert_hidden, h=h))
        for i in (2 * h, 2 * h + 1):
            weight_copy(FAR, i).wait_recv()
        pl.loop(FAR, FAR + 1)(functools.partial(expert_hidden, h=h))

    for t in range(dn_pieces):
        weight_copy(CHIP, gu_pieces + t).wait_recv()
        weight_copy(FAR, gu_pieces + t).start()
        weight_copy(CORE, gu_pieces + t).wait_recv()
        weight_copy(FAR, gu_pieces + t).wait_recv()
        cols = pl.ds(t * TILE, TILE)
        for which in (1, 0):
            part = pl.ds(which * half_rows, half_rows)
            result_buf[part, cols] = jnp.dot(
                hidden[part, :], dn_buf[:, cols], preferred_element_type=F32
            ).astype(BF16)

            @pl.loop(max(1, which * half), which * half + half)
            def _(d):
                back_copy(d, t).start()

    back_buf[rows_at(me * cap, cap), :] = result_buf[pl.ds(0, cap), :]

    @pl.loop(0, dn_pieces)
    def _(t):
        @pl.loop(1, n_exp)
        def _(d):
            back_copy(d, t).wait_recv()

        cols = columns_at(t, TILE)
        total = mixed[:, cols].astype(F32)
        for j in range(top):
            routed = jnp.dot(pick[j], back_buf[:, cols], preferred_element_type=F32)
            total = total + gate_column[j, :, 0:1] * routed
        out_ref[:, cols] = total.astype(BF16)

    @pl.loop(1, n_exp)
    def _(d):
        out_copy(d).wait_send()
        for t in range(dn_pieces):
            back_copy(d, t).wait_send()

    @pl.loop(0, chunks)
    def _(g):
        for kind in range(2):
            for route in (CORE, CHIP, FAR):
                kv_copy(kind, route, g).wait_send()

    for i in range(pieces):
        for route in (CORE, CHIP, FAR):
            weight_copy(route, i).wait_send()


def shards(
    queries,
    key_rows,
    value_rows,
    residual_in,
    norm_gain,
    routes,
    gate_weights,
    gate_up_weight,
    down_weight,
):
    clip_count, row_count, feature_count = queries.shape
    tokens = clip_count * row_count
    top = routes.shape[-1]
    n_exp = lax.axis_size("exp")
    n_ctx = lax.axis_size("ctx")
    units = down_weight.shape[1]
    assert clip_count == 1 and n_ctx == 4 and gate_up_weight.shape[0] == 1
    assert n_exp & (n_exp - 1) == 0 and feature_count == HEADS * 128
    capacity = max(2, -(-(5 * tokens * top) // (4 * n_exp)))
    cap = -(-capacity // 16) * 16
    slots = n_exp * cap
    chunk = 256
    chunks = feature_count // chunk
    tiles = feature_count // TILE
    flat = (tokens, feature_count)
    anywhere = pl.BlockSpec(memory_space=pl.ANY)
    vmem = pl.BlockSpec(memory_space=pltpu.VMEM)
    dma = pltpu.SemaphoreType.DMA
    out = pl.pallas_call(
        functools.partial(layer_kernel, n_exp, cap, chunk, (feature_count // HEADS) ** (-0.5)),
        out_shape=jax.ShapeDtypeStruct(flat, BF16),
        in_specs=[anywhere] * 4 + [vmem] * 3 + [anywhere] * 2,
        out_specs=vmem,
        scratch_shapes=[
            pltpu.VMEM(flat, BF16),
            pltpu.VMEM((n_ctx * tokens, feature_count), BF16),
            pltpu.VMEM((n_ctx * tokens, feature_count), BF16),
            pltpu.VMEM(flat, BF16),
            pltpu.VMEM(flat, BF16),
            pltpu.VMEM((feature_count, 2, units), BF16),
            pltpu.VMEM((n_ctx, feature_count, 2 * units), BF16),
            pltpu.VMEM((n_ctx * units, feature_count), BF16),
            pltpu.VMEM((top, tokens, slots), BF16),
            pltpu.VMEM((slots, tokens), BF16),
            pltpu.VMEM((top, tokens, 128), F32),
            pltpu.VMEM((slots, feature_count), BF16),
            pltpu.VMEM((slots, feature_count), BF16),
            pltpu.VMEM((slots, n_ctx * units), BF16),
            pltpu.VMEM((slots, feature_count), BF16),
            pltpu.VMEM((slots, feature_count), BF16),
            dma((6,)),
            dma((2, 3, chunks)),
            dma((2, 3, chunks)),
            dma((3, 4 + tiles)),
            dma((3, 4 + tiles)),
            dma((n_exp,)),
            dma((n_exp,)),
            dma((n_exp, tiles)),
            dma((n_exp, tiles)),
        ],
        compiler_params=pltpu.CompilerParams(
            collective_id=0, has_side_effects=True, vmem_limit_bytes=60 * 1024 * 1024
        ),
        cost_estimate=pl.CostEstimate(
            flops=10_000_000_000, bytes_accessed=20_000_000, transcendentals=5_000_000
        ),
    )(
        queries.reshape(flat),
        key_rows.reshape(flat),
        value_rows.reshape(flat),
        residual_in.reshape(flat),
        norm_gain.reshape(1, feature_count),
        routes.reshape(tokens, top).T,
        gate_weights.reshape(tokens, top).T,
        gate_up_weight.reshape(feature_count, 2, units),
        down_weight.reshape(units, feature_count),
    )
    return out.reshape(clip_count, row_count, feature_count)


def solution(mesh):
    return jax.shard_map(
        shards,
        mesh=mesh,
        in_specs=(
            P("exp", "ctx", None),
            P("exp", "ctx", None),
            P("exp", "ctx", None),
            P("exp", "ctx", None),
            P(),
            P("exp", "ctx", None),
            P("exp", "ctx", None),
            P("exp", None, None, "ctx"),
            P("exp", "ctx", None),
        ),
        out_specs=P("exp", "ctx", None),
        check_vma=False,
    )
```

```python
import functools

import jax
import jax.numpy as jnp
from jax import lax
from jax.experimental import pallas as pl
from jax.experimental.pallas import tpu as pltpu
from jax.sharding import PartitionSpec as P

HEADS = 16
MESH = pl.DeviceIdType.MESH
F32 = jnp.float32
BF16 = jnp.bfloat16
OWN, CORE, CHIP, FAR = range(4)
TILE = 512
AHEAD = 3


def flipped(index, offset, extent):
    result = jnp.int32(0)
    bit = 1
    while bit < extent:
        both = lax.div(index, jnp.int32(bit)) + lax.div(jnp.int32(offset), jnp.int32(bit))
        result = result + lax.rem(both, jnp.int32(2)) * bit
        bit *= 2
    return result


def rows_at(start, count):
    return pl.ds(pl.multiple_of(start, 16), count)


def columns_at(step, width):
    return pl.ds(pl.multiple_of(step * width, width), width)


def layer_kernel(
    n_exp, cap, chunk, scale,
    q_ref, k_ref, v_ref, residual_ref, gain_ref, routes_ref, gates_ref, gu_ref, dn_ref,
    out_ref,
    q_buf, k_buf, v_buf, residual_buf, mixed, raw_buf, gu_buf, dn_buf,
    pick, place, gate_column, send_buf, recv_buf, hidden, result_buf, back_buf,
    local_sem, kv_send, kv_recv, w_send, w_recv, out_send, out_recv, back_send, back_recv,
):
    tokens, features = q_ref.shape
    top = gates_ref.shape[0]
    units = dn_ref.shape[0]
    half_units = units // 2
    slots = send_buf.shape[0]
    chunks = features // chunk
    half = n_exp // 2
    half_rows = half * cap
    ctx = lax.axis_index("ctx")
    me = lax.axis_index("exp")
    core_peer = flipped(ctx, 1, 4)
    chip_peer = flipped(ctx, 2, 4)
    far_peer = flipped(ctx, 3, 4)

    local = [
        pltpu.make_async_copy(src, dst, local_sem.at[i])
        for i, (src, dst) in enumerate(
            [
                (q_ref, q_buf),
                (k_ref, k_buf.at[pl.ds(0, tokens)]),
                (v_ref, v_buf.at[pl.ds(0, tokens)]),
                (residual_ref, residual_buf),
                (gu_ref, raw_buf),
                (dn_ref, dn_buf.at[pl.ds(0, units)]),
            ]
        )
    ]
    for copy in local:
        copy.start()

    barrier = pltpu.get_barrier_semaphore()
    for peer in (core_peer, chip_peer, far_peer):
        pl.semaphore_signal(barrier, inc=1, device_id={"ctx": peer}, device_id_type=MESH)

    @pl.loop(1, n_exp)
    def _(d):
        pl.semaphore_signal(
            barrier, inc=1, device_id={"exp": flipped(me, d, n_exp)}, device_id_type=MESH
        )

    pl.semaphore_wait(barrier, 3 + n_exp - 1)

    def kv_copy(kind, route, g):
        src, buf = ((k_ref, k_buf), (v_ref, v_buf))[kind]
        cols = columns_at(g, chunk)
        if route == FAR:
            block = buf.at[pl.ds(CHIP * tokens, tokens), cols]
        else:
            block = src.at[:, cols]
        return pltpu.make_async_remote_copy(
            src_ref=block,
            dst_ref=buf.at[pl.ds(route * tokens, tokens), cols],
            send_sem=kv_send.at[kind, route - 1, g],
            recv_sem=kv_recv.at[kind, route - 1, g],
            device_id={"ctx": chip_peer if route == CHIP else core_peer},
            device_id_type=MESH,
        )

    gu_pieces, dn_pieces = 4, features // TILE
    pieces = gu_pieces + dn_pieces

    def weight_copy(route, i):
        if i < gu_pieces:
            part = pl.ds(i % 2 * (features // 2), features // 2)
            cols = pl.ds(i // 2 * units, units)
            src, dst = gu_buf.at[OWN, part, cols], gu_buf.at[route, part, cols]
            held = gu_buf.at[CHIP, part, cols]
        else:
            cols = pl.ds((i - gu_pieces) * TILE, TILE)
            src = dn_ref.at[:, cols]
            dst = dn_buf.at[pl.ds(route * units, units), cols]
            held = dn_buf.at[pl.ds(CHIP * units, units), cols]
        return pltpu.make_async_remote_copy(
            src_ref=held if route == FAR else src,
            dst_ref=dst,
            send_sem=w_send.at[route - 1, i],
            recv_sem=w_recv.at[route - 1, i],
            device_id={"ctx": chip_peer if route == CHIP else core_peer},
            device_id_type=MESH,
        )

    @pl.loop(0, AHEAD)
    def _(g):
        for kind in range(2):
            kv_copy(kind, CHIP, g).start()

    @pl.loop(0, chunks)
    def _(g):
        for kind in range(2):
            kv_copy(kind, CORE, g).start()

    local[4].wait()

    @pl.loop(0, features // 128)
    def _(i):
        part = rows_at(i * 128, 128)
        for j in range(2):
            value = raw_buf[part, j, :]
            for h in range(2):
                gu_buf[OWN, part, h * units + j * half_units : h * units + (j + 1) * half_units] = (
                    value[:, h * half_units : (h + 1) * half_units]
                )

    for i in range(pieces):
        weight_copy(CORE, i).start()

    expert_row = lax.broadcasted_iota(jnp.int32, (128, tokens), 0)
    named = [routes_ref[j : j + 1, :] == expert_row for j in range(top)]
    counted = sum(jnp.where(hit, 1.0, 0.0) for hit in named).astype(BF16)
    row = lax.broadcasted_iota(jnp.int32, (tokens, tokens), 0)
    col = lax.broadcasted_iota(jnp.int32, (tokens, tokens), 1)
    earlier = jnp.where(row < col, 1.0, 0.0).astype(BF16)
    slot = jnp.dot(counted, earlier, preferred_element_type=F32) + (expert_row * cap).astype(F32)
    slot_row = lax.broadcasted_iota(jnp.int32, (slots, tokens), 0).astype(F32)
    slot_lane = lax.broadcasted_iota(jnp.int32, (tokens, slots), 1).astype(F32)
    placed = jnp.zeros((slots, tokens), F32)
    for j in range(top):
        target = jnp.sum(jnp.where(named[j], slot, 0.0), axis=0, keepdims=True)
        placed = placed + jnp.where(target == slot_row, 1.0, 0.0)
        target = jnp.sum(jnp.where(row == col, target, 0.0), axis=1, keepdims=True)
        pick[j] = jnp.where(target == slot_lane, 1.0, 0.0).astype(BF16)
        gate = jnp.sum(jnp.where(row == col, gates_ref[j : j + 1, :], 0.0), axis=1, keepdims=True)
        gate_column[j] = jnp.broadcast_to(gate, (tokens, 128))
    place[...] = placed.astype(BF16)

    for i in (0, 1, 2, 3, 5):
        local[i].wait()

    def out_copy(d, cols=slice(None)):
        return pltpu.make_async_remote_copy(
            src_ref=send_buf.at[rows_at(flipped(me, d, n_exp) * cap, cap), cols],
            dst_ref=recv_buf.at[rows_at(d * cap, cap), cols],
            send_sem=out_send.at[d],
            recv_sem=out_recv.at[d],
            device_id={"exp": flipped(me, d, n_exp)},
            device_id_type=MESH,
        )

    def back_copy(d, t):
        cols = columns_at(t, TILE)
        return pltpu.make_async_remote_copy(
            src_ref=result_buf.at[rows_at(d * cap, cap), cols],
            dst_ref=back_buf.at[rows_at(me * cap, cap), cols],
            send_sem=back_send.at[d, t],
            recv_sem=back_recv.at[d, t],
            device_id={"exp": flipped(me, d, n_exp)},
            device_id_type=MESH,
        )

    @pl.loop(0, chunks + 1)
    def _(g):
        @pl.when(g < chunks)
        def _():
            for kind in range(2):
                kv_copy(kind, CHIP, g).wait_recv()
                kv_copy(kind, FAR, g).start()

        @pl.when(g + AHEAD < chunks)
        def _():
            for kind in range(2):
                kv_copy(kind, CHIP, g + AHEAD).start()

        for i in range(AHEAD):

            @pl.when(g == chunks - AHEAD + i)
            def _():
                weight_copy(CHIP, i).start()

        @pl.when(g > 0)
        def _():
            done = g - 1
            for kind in range(2):
                kv_copy(kind, CORE, done).wait_recv()
                kv_copy(kind, FAR, done).wait_recv()
            for h in range(chunk // 128):
                cols = pl.ds(pl.multiple_of(done * chunk + h * 128, 128), 128)
                scores = (
                    lax.dot_general(
                        q_buf[:, cols], k_buf[:, cols], (((1,), (1,)), ((), ())),
                        preferred_element_type=F32,
                    )
                    * scale
                )
                expo = jnp.exp(scores - jnp.max(scores, axis=1, keepdims=True))
                total = jnp.sum(expo, axis=1, keepdims=True)
                weighted = jnp.dot(expo.astype(BF16), v_buf[:, cols], preferred_element_type=F32)
                mixed[:, cols] = (residual_buf[:, cols].astype(F32) + weighted / total).astype(BF16)

            cols = columns_at(done, chunk)
            send_buf[:, cols] = jnp.dot(
                place[...], mixed[:, cols], preferred_element_type=F32
            ).astype(BF16)

            @pl.loop(1, n_exp)
            def _(d):
                out_copy(n_exp - d, cols).start()

    def weight_step(i, following):
        weight_copy(CHIP, i).wait_recv()
        weight_copy(FAR, i).start()
        for n in following:
            weight_copy(CHIP, n).start()

    weight_step(0, [3])
    weight_step(1, [])

    recv_buf[pl.ds(0, cap), :] = send_buf[rows_at(me * cap, cap), :]

    @pl.loop(1, n_exp)
    def _(d):
        out_copy(d).wait_recv()

    @pl.loop(0, slots // 16)
    def _(i):
        part = rows_at(i * 16, 16)
        value = recv_buf[part, :].astype(F32)
        mean_square = jnp.mean(value * value, axis=1, keepdims=True)
        recv_buf[part, :] = (value * lax.rsqrt(mean_square + 1e-05) * gain_ref[...]).astype(BF16)

    def expert_hidden(r, h):
        both = jnp.dot(
            recv_buf[...], gu_buf[r, :, h * units : (h + 1) * units], preferred_element_type=F32
        )
        gate, up = both[:, :half_units], both[:, half_units:]
        cols = columns_at(2 * r + h, half_units)
        hidden[:, cols] = (gate / (1.0 + jnp.exp(-gate)) * up).astype(BF16)

    for i in range(gu_pieces):
        weight_copy(CORE, i).wait_recv()

    @pl.loop(OWN, CHIP)
    def _(r):
        expert_hidden(r, 0)
        expert_hidden(r, 1)

    for h in range(2):
        if h == 1:
            weight_step(2, [gu_pieces])
            weight_step(3, range(gu_pieces + 1, pieces))
        pl.loop(CHIP, CHIP + 1)(functools.partial(expert_hidden, h=h))
        for i in (2 * h, 2 * h + 1):
            weight_copy(FAR, i).wait_recv()
        pl.loop(FAR, FAR + 1)(functools.partial(expert_hidden, h=h))

    for t in range(dn_pieces):
        weight_copy(CHIP, gu_pieces + t).wait_recv()
        weight_copy(FAR, gu_pieces + t).start()
        weight_copy(CORE, gu_pieces + t).wait_recv()
        weight_copy(FAR, gu_pieces + t).wait_recv()
        cols = pl.ds(t * TILE, TILE)
        for which in (1, 0):
            part = pl.ds(which * half_rows, half_rows)
            result_buf[part, cols] = jnp.dot(
                hidden[part, :], dn_buf[:, cols], preferred_element_type=F32
            ).astype(BF16)

            @pl.loop(max(1, which * half), which * half + half)
            def _(d):
                back_copy(d, t).start()

    back_buf[rows_at(me * cap, cap), :] = result_buf[pl.ds(0, cap), :]

    @pl.loop(0, dn_pieces)
    def _(t):
        @pl.loop(1, n_exp)
        def _(d):
            back_copy(d, t).wait_recv()

        cols = columns_at(t, TILE)
        total = mixed[:, cols].astype(F32)
        for j in range(top):
            routed = jnp.dot(pick[j], back_buf[:, cols], preferred_element_type=F32)
            total = total + gate_column[j, :, 0:1] * routed
        out_ref[:, cols] = total.astype(BF16)

    @pl.loop(1, n_exp)
    def _(d):
        out_copy(d).wait_send()
        for t in range(dn_pieces):
            back_copy(d, t).wait_send()

    @pl.loop(0, chunks)
    def _(g):
        for kind in range(2):
            for route in (CORE, CHIP, FAR):
                kv_copy(kind, route, g).wait_send()

    for i in range(pieces):
        for route in (CORE, CHIP, FAR):
            weight_copy(route, i).wait_send()


def shards(
    queries,
    key_rows,
    value_rows,
    residual_in,
    norm_gain,
    routes,
    gate_weights,
    gate_up_weight,
    down_weight,
):
    clip_count, row_count, feature_count = queries.shape
    tokens = clip_count * row_count
    top = routes.shape[-1]
    n_exp = lax.axis_size("exp")
    n_ctx = lax.axis_size("ctx")
    units = down_weight.shape[1]
    assert clip_count == 1 and n_ctx == 4 and gate_up_weight.shape[0] == 1
    assert n_exp & (n_exp - 1) == 0 and feature_count == HEADS * 128
    capacity = max(2, -(-(5 * tokens * top) // (4 * n_exp)))
    cap = -(-capacity // 16) * 16
    slots = n_exp * cap
    chunk = 256
    chunks = feature_count // chunk
    tiles = feature_count // TILE
    flat = (tokens, feature_count)
    anywhere = pl.BlockSpec(memory_space=pl.ANY)
    vmem = pl.BlockSpec(memory_space=pltpu.VMEM)
    dma = pltpu.SemaphoreType.DMA
    out = pl.pallas_call(
        functools.partial(layer_kernel, n_exp, cap, chunk, (feature_count // HEADS) ** (-0.5)),
        out_shape=jax.ShapeDtypeStruct(flat, BF16),
        in_specs=[anywhere] * 4 + [vmem] * 3 + [anywhere] * 2,
        out_specs=vmem,
        scratch_shapes=[
            pltpu.VMEM(flat, BF16),
            pltpu.VMEM((n_ctx * tokens, feature_count), BF16),
            pltpu.VMEM((n_ctx * tokens, feature_count), BF16),
            pltpu.VMEM(flat, BF16),
            pltpu.VMEM(flat, BF16),
            pltpu.VMEM((feature_count, 2, units), BF16),
            pltpu.VMEM((n_ctx, feature_count, 2 * units), BF16),
            pltpu.VMEM((n_ctx * units, feature_count), BF16),
            pltpu.VMEM((top, tokens, slots), BF16),
            pltpu.VMEM((slots, tokens), BF16),
            pltpu.VMEM((top, tokens, 128), F32),
            pltpu.VMEM((slots, feature_count), BF16),
            pltpu.VMEM((slots, feature_count), BF16),
            pltpu.VMEM((slots, n_ctx * units), BF16),
            pltpu.VMEM((slots, feature_count), BF16),
            pltpu.VMEM((slots, feature_count), BF16),
            dma((6,)),
            dma((2, 3, chunks)),
            dma((2, 3, chunks)),
            dma((3, 4 + tiles)),
            dma((3, 4 + tiles)),
            dma((n_exp,)),
            dma((n_exp,)),
            dma((n_exp, tiles)),
            dma((n_exp, tiles)),
        ],
        compiler_params=pltpu.CompilerParams(
            collective_id=0, has_side_effects=True, vmem_limit_bytes=60 * 1024 * 1024
        ),
        cost_estimate=pl.CostEstimate(
            flops=10_000_000_000, bytes_accessed=20_000_000, transcendentals=5_000_000
        ),
    )(
        queries.reshape(flat),
        key_rows.reshape(flat),
        value_rows.reshape(flat),
        residual_in.reshape(flat),
        norm_gain.reshape(1, feature_count),
        routes.reshape(tokens, top).T,
        gate_weights.reshape(tokens, top).T,
        gate_up_weight.reshape(feature_count, 2, units),
        down_weight.reshape(units, feature_count),
    )
    return out.reshape(clip_count, row_count, feature_count)


def solution(mesh):
    return jax.shard_map(
        shards,
        mesh=mesh,
        in_specs=(
            P("exp", "ctx", None),
            P("exp", "ctx", None),
            P("exp", "ctx", None),
            P("exp", "ctx", None),
            P(),
            P("exp", "ctx", None),
            P("exp", "ctx", None),
            P("exp", None, None, "ctx"),
            P("exp", "ctx", None),
        ),
        out_specs=P("exp", "ctx", None),
        check_vma=False,
    )
```

```python
import functools

import jax
import jax.numpy as jnp
from jax import lax
from jax.experimental import pallas as pl
from jax.experimental.pallas import tpu as pltpu
from jax.sharding import PartitionSpec as P

HEADS = 16
MESH = pl.DeviceIdType.MESH
F32 = jnp.float32
BF16 = jnp.bfloat16
OWN, CORE, CHIP, FAR = range(4)
TILE = 512
AHEAD = 3


def flipped(index, offset, extent):
    result = jnp.int32(0)
    bit = 1
    while bit < extent:
        both = lax.div(index, jnp.int32(bit)) + lax.div(jnp.int32(offset), jnp.int32(bit))
        result = result + lax.rem(both, jnp.int32(2)) * bit
        bit *= 2
    return result


def rows_at(start, count):
    return pl.ds(pl.multiple_of(start, 16), count)


def columns_at(step, width):
    return pl.ds(pl.multiple_of(step * width, width), width)


def layer_kernel(
    n_exp, cap, chunk, scale,
    q_ref, k_ref, v_ref, residual_ref, gain_ref, routes_ref, gates_ref, gu_ref, dn_ref,
    out_ref,
    q_buf, k_buf, v_buf, residual_buf, mixed, raw_buf, gu_buf, dn_buf,
    pick, place, gate_column, send_buf, recv_buf, hidden, result_buf, back_buf,
    local_sem, kv_send, kv_recv, w_send, w_recv, out_send, out_recv, back_send, back_recv,
):
    tokens, features = q_ref.shape
    top = gates_ref.shape[0]
    units = dn_ref.shape[0]
    half_units = units // 2
    slots = send_buf.shape[0]
    chunks = features // chunk
    half = n_exp // 2
    half_rows = half * cap
    ctx = lax.axis_index("ctx")
    me = lax.axis_index("exp")
    core_peer = flipped(ctx, 1, 4)
    chip_peer = flipped(ctx, 2, 4)
    far_peer = flipped(ctx, 3, 4)

    local = [
        pltpu.make_async_copy(src, dst, local_sem.at[i])
        for i, (src, dst) in enumerate(
            [
                (q_ref, q_buf),
                (k_ref, k_buf.at[pl.ds(0, tokens)]),
                (v_ref, v_buf.at[pl.ds(0, tokens)]),
                (residual_ref, residual_buf),
                (gu_ref, raw_buf),
                (dn_ref, dn_buf.at[pl.ds(0, units)]),
            ]
        )
    ]
    for copy in local:
        copy.start()

    barrier = pltpu.get_barrier_semaphore()
    for peer in (core_peer, chip_peer, far_peer):
        pl.semaphore_signal(barrier, inc=1, device_id={"ctx": peer}, device_id_type=MESH)

    @pl.loop(1, n_exp)
    def _(d):
        pl.semaphore_signal(
            barrier, inc=1, device_id={"exp": flipped(me, d, n_exp)}, device_id_type=MESH
        )

    pl.semaphore_wait(barrier, 3 + n_exp - 1)

    def kv_copy(kind, route, g):
        src, buf = ((k_ref, k_buf), (v_ref, v_buf))[kind]
        cols = columns_at(g, chunk)
        if route == FAR:
            block = buf.at[pl.ds(CHIP * tokens, tokens), cols]
        else:
            block = src.at[:, cols]
        return pltpu.make_async_remote_copy(
            src_ref=block,
            dst_ref=buf.at[pl.ds(route * tokens, tokens), cols],
            send_sem=kv_send.at[kind, route - 1, g],
            recv_sem=kv_recv.at[kind, route - 1, g],
            device_id={"ctx": chip_peer if route == CHIP else core_peer},
            device_id_type=MESH,
        )

    gu_pieces, dn_pieces = 4, features // TILE
    pieces = gu_pieces + dn_pieces

    def weight_copy(route, i):
        if i < gu_pieces:
            part = pl.ds(i % 2 * (features // 2), features // 2)
            cols = pl.ds(i // 2 * units, units)
            src, dst = gu_buf.at[OWN, part, cols], gu_buf.at[route, part, cols]
            held = gu_buf.at[CHIP, part, cols]
        else:
            cols = pl.ds((i - gu_pieces) * TILE, TILE)
            src = dn_ref.at[:, cols]
            dst = dn_buf.at[pl.ds(route * units, units), cols]
            held = dn_buf.at[pl.ds(CHIP * units, units), cols]
        return pltpu.make_async_remote_copy(
            src_ref=held if route == FAR else src,
            dst_ref=dst,
            send_sem=w_send.at[route - 1, i],
            recv_sem=w_recv.at[route - 1, i],
            device_id={"ctx": chip_peer if route == CHIP else core_peer},
            device_id_type=MESH,
        )

    @pl.loop(0, AHEAD)
    def _(g):
        for kind in range(2):
            kv_copy(kind, CHIP, g).start()

    @pl.loop(0, chunks)
    def _(g):
        for kind in range(2):
            kv_copy(kind, CORE, g).start()

    local[4].wait()

    @pl.loop(0, features // 128)
    def _(i):
        part = rows_at(i * 128, 128)
        for j in range(2):
            value = raw_buf[part, j, :]
            for h in range(2):
                gu_buf[OWN, part, h * units + j * half_units : h * units + (j + 1) * half_units] = (
                    value[:, h * half_units : (h + 1) * half_units]
                )

    for i in range(pieces):
        weight_copy(CORE, i).start()

    expert_row = lax.broadcasted_iota(jnp.int32, (128, tokens), 0)
    named = [routes_ref[j : j + 1, :] == expert_row for j in range(top)]
    counted = sum(jnp.where(hit, 1.0, 0.0) for hit in named).astype(BF16)
    row = lax.broadcasted_iota(jnp.int32, (tokens, tokens), 0)
    col = lax.broadcasted_iota(jnp.int32, (tokens, tokens), 1)
    earlier = jnp.where(row < col, 1.0, 0.0).astype(BF16)
    slot = jnp.dot(counted, earlier, preferred_element_type=F32) + (expert_row * cap).astype(F32)
    slot_row = lax.broadcasted_iota(jnp.int32, (slots, tokens), 0).astype(F32)
    slot_lane = lax.broadcasted_iota(jnp.int32, (tokens, slots), 1).astype(F32)
    placed = jnp.zeros((slots, tokens), F32)
    for j in range(top):
        target = jnp.sum(jnp.where(named[j], slot, 0.0), axis=0, keepdims=True)
        placed = placed + jnp.where(target == slot_row, 1.0, 0.0)
        target = jnp.sum(jnp.where(row == col, target, 0.0), axis=1, keepdims=True)
        pick[j] = jnp.where(target == slot_lane, 1.0, 0.0).astype(BF16)
        gate = jnp.sum(jnp.where(row == col, gates_ref[j : j + 1, :], 0.0), axis=1, keepdims=True)
        gate_column[j] = jnp.broadcast_to(gate, (tokens, 128))
    place[...] = placed.astype(BF16)

    for i in (0, 1, 2, 3, 5):
        local[i].wait()

    def out_copy(d, cols=slice(None)):
        return pltpu.make_async_remote_copy(
            src_ref=send_buf.at[rows_at(flipped(me, d, n_exp) * cap, cap), cols],
            dst_ref=recv_buf.at[rows_at(d * cap, cap), cols],
            send_sem=out_send.at[d],
            recv_sem=out_recv.at[d],
            device_id={"exp": flipped(me, d, n_exp)},
            device_id_type=MESH,
        )

    def back_copy(d, t):
        cols = columns_at(t, TILE)
        return pltpu.make_async_remote_copy(
            src_ref=result_buf.at[rows_at(d * cap, cap), cols],
            dst_ref=back_buf.at[rows_at(me * cap, cap), cols],
            send_sem=back_send.at[d, t],
            recv_sem=back_recv.at[d, t],
            device_id={"exp": flipped(me, d, n_exp)},
            device_id_type=MESH,
        )

    @pl.loop(0, chunks + 1)
    def _(g):
        @pl.when(g < chunks)
        def _():
            for kind in range(2):
                kv_copy(kind, CHIP, g).wait_recv()
                kv_copy(kind, FAR, g).start()

        @pl.when(g + AHEAD < chunks)
        def _():
            for kind in range(2):
                kv_copy(kind, CHIP, g + AHEAD).start()

        for i in range(AHEAD):

            @pl.when(g == chunks - AHEAD + i)
            def _():
                weight_copy(CHIP, i).start()

        @pl.when(g > 0)
        def _():
            done = g - 1
            for kind in range(2):
                kv_copy(kind, CORE, done).wait_recv()
                kv_copy(kind, FAR, done).wait_recv()
            for h in range(chunk // 128):
                cols = pl.ds(pl.multiple_of(done * chunk + h * 128, 128), 128)
                scores = (
                    lax.dot_general(
                        q_buf[:, cols], k_buf[:, cols], (((1,), (1,)), ((), ())),
                        preferred_element_type=F32,
                    )
                    * scale
                )
                expo = jnp.exp(scores - jnp.max(scores, axis=1, keepdims=True))
                total = jnp.sum(expo, axis=1, keepdims=True)
                weighted = jnp.dot(expo.astype(BF16), v_buf[:, cols], preferred_element_type=F32)
                mixed[:, cols] = (residual_buf[:, cols].astype(F32) + weighted / total).astype(BF16)

            cols = columns_at(done, chunk)
            send_buf[:, cols] = jnp.dot(
                place[...], mixed[:, cols], preferred_element_type=F32
            ).astype(BF16)

            @pl.loop(1, n_exp)
            def _(d):
                out_copy(n_exp - d, cols).start()

    def weight_step(i, following):
        weight_copy(CHIP, i).wait_recv()
        weight_copy(FAR, i).start()
        for n in following:
            weight_copy(CHIP, n).start()

    weight_step(0, [3])
    weight_step(1, [])

    recv_buf[pl.ds(0, cap), :] = send_buf[rows_at(me * cap, cap), :]

    @pl.loop(1, n_exp)
    def _(d):
        out_copy(d).wait_recv()

    @pl.loop(0, slots // 32)
    def _(i):
        part = rows_at(i * 32, 32)
        value = recv_buf[part, :].astype(F32)
        mean_square = jnp.mean(value * value, axis=1, keepdims=True)
        recv_buf[part, :] = (value * lax.rsqrt(mean_square + 1e-05) * gain_ref[...]).astype(BF16)

    def expert_hidden(r, h):
        both = jnp.dot(
            recv_buf[...], gu_buf[r, :, h * units : (h + 1) * units], preferred_element_type=F32
        )
        gate, up = both[:, :half_units], both[:, half_units:]
        cols = columns_at(2 * r + h, half_units)
        hidden[:, cols] = (gate / (1.0 + jnp.exp(-gate)) * up).astype(BF16)

    for i in range(gu_pieces):
        weight_copy(CORE, i).wait_recv()

    @pl.loop(OWN, CHIP)
    def _(r):
        expert_hidden(r, 0)
        expert_hidden(r, 1)

    for h in range(2):
        if h == 1:
            weight_step(2, [gu_pieces])
            weight_step(3, range(gu_pieces + 1, pieces))
        pl.loop(CHIP, CHIP + 1)(functools.partial(expert_hidden, h=h))
        for i in (2 * h, 2 * h + 1):
            weight_copy(FAR, i).wait_recv()
        pl.loop(FAR, FAR + 1)(functools.partial(expert_hidden, h=h))

    def send_results(which, t):
        part = pl.ds(which * half_rows, half_rows)
        cols = columns_at(t, TILE)
        result_buf[part, cols] = jnp.dot(
            hidden[part, :], dn_buf[:, cols], preferred_element_type=F32
        ).astype(BF16)

        @pl.loop(max(1, which * half), which * half + half)
        def _(d):
            back_copy(d, t).start()

    for t in range(dn_pieces):
        weight_copy(CHIP, gu_pieces + t).wait_recv()
        weight_copy(FAR, gu_pieces + t).start()
        weight_copy(CORE, gu_pieces + t).wait_recv()
        weight_copy(FAR, gu_pieces + t).wait_recv()
        send_results(1, t)

    @pl.loop(0, dn_pieces)
    def _(t):
        send_results(0, t)

    back_buf[rows_at(me * cap, cap), :] = result_buf[pl.ds(0, cap), :]

    @pl.loop(0, dn_pieces)
    def _(t):
        @pl.loop(1, n_exp)
        def _(d):
            back_copy(d, t).wait_recv()

        cols = columns_at(t, TILE)
        total = mixed[:, cols].astype(F32)
        for j in range(top):
            routed = jnp.dot(pick[j], back_buf[:, cols], preferred_element_type=F32)
            total = total + gate_column[j, :, 0:1] * routed
        out_ref[:, cols] = total.astype(BF16)

    @pl.loop(1, n_exp)
    def _(d):
        out_copy(d).wait_send()
        for t in range(dn_pieces):
            back_copy(d, t).wait_send()

    @pl.loop(0, chunks)
    def _(g):
        for kind in range(2):
            for route in (CORE, CHIP, FAR):
                kv_copy(kind, route, g).wait_send()

    for i in range(pieces):
        for route in (CORE, CHIP, FAR):
            weight_copy(route, i).wait_send()


def shards(
    queries,
    key_rows,
    value_rows,
    residual_in,
    norm_gain,
    routes,
    gate_weights,
    gate_up_weight,
    down_weight,
):
    clip_count, row_count, feature_count = queries.shape
    tokens = clip_count * row_count
    top = routes.shape[-1]
    n_exp = lax.axis_size("exp")
    n_ctx = lax.axis_size("ctx")
    units = down_weight.shape[1]
    assert clip_count == 1 and n_ctx == 4 and gate_up_weight.shape[0] == 1
    assert n_exp & (n_exp - 1) == 0 and feature_count == HEADS * 128
    capacity = max(2, -(-(5 * tokens * top) // (4 * n_exp)))
    cap = -(-capacity // 16) * 16
    slots = n_exp * cap
    chunk = 256
    chunks = feature_count // chunk
    tiles = feature_count // TILE
    flat = (tokens, feature_count)
    anywhere = pl.BlockSpec(memory_space=pl.ANY)
    vmem = pl.BlockSpec(memory_space=pltpu.VMEM)
    dma = pltpu.SemaphoreType.DMA
    out = pl.pallas_call(
        functools.partial(layer_kernel, n_exp, cap, chunk, (feature_count // HEADS) ** (-0.5)),
        out_shape=jax.ShapeDtypeStruct(flat, BF16),
        in_specs=[anywhere] * 4 + [vmem] * 3 + [anywhere] * 2,
        out_specs=vmem,
        scratch_shapes=[
            pltpu.VMEM(flat, BF16),
            pltpu.VMEM((n_ctx * tokens, feature_count), BF16),
            pltpu.VMEM((n_ctx * tokens, feature_count), BF16),
            pltpu.VMEM(flat, BF16),
            pltpu.VMEM(flat, BF16),
            pltpu.VMEM((feature_count, 2, units), BF16),
            pltpu.VMEM((n_ctx, feature_count, 2 * units), BF16),
            pltpu.VMEM((n_ctx * units, feature_count), BF16),
            pltpu.VMEM((top, tokens, slots), BF16),
            pltpu.VMEM((slots, tokens), BF16),
            pltpu.VMEM((top, tokens, 128), F32),
            pltpu.VMEM((slots, feature_count), BF16),
            pltpu.VMEM((slots, feature_count), BF16),
            pltpu.VMEM((slots, n_ctx * units), BF16),
            pltpu.VMEM((slots, feature_count), BF16),
            pltpu.VMEM((slots, feature_count), BF16),
            dma((6,)),
            dma((2, 3, chunks)),
            dma((2, 3, chunks)),
            dma((3, 4 + tiles)),
            dma((3, 4 + tiles)),
            dma((n_exp,)),
            dma((n_exp,)),
            dma((n_exp, tiles)),
            dma((n_exp, tiles)),
        ],
        compiler_params=pltpu.CompilerParams(
            collective_id=0, has_side_effects=True, vmem_limit_bytes=60 * 1024 * 1024
        ),
        cost_estimate=pl.CostEstimate(
            flops=10_000_000_000, bytes_accessed=20_000_000, transcendentals=5_000_000
        ),
    )(
        queries.reshape(flat),
        key_rows.reshape(flat),
        value_rows.reshape(flat),
        residual_in.reshape(flat),
        norm_gain.reshape(1, feature_count),
        routes.reshape(tokens, top).T,
        gate_weights.reshape(tokens, top).T,
        gate_up_weight.reshape(feature_count, 2, units),
        down_weight.reshape(units, feature_count),
    )
    return out.reshape(clip_count, row_count, feature_count)


def solution(mesh):
    return jax.shard_map(
        shards,
        mesh=mesh,
        in_specs=(
            P("exp", "ctx", None),
            P("exp", "ctx", None),
            P("exp", "ctx", None),
            P("exp", "ctx", None),
            P(),
            P("exp", "ctx", None),
            P("exp", "ctx", None),
            P("exp", None, None, "ctx"),
            P("exp", "ctx", None),
        ),
        out_specs=P("exp", "ctx", None),
        check_vma=False,
    )
```
